128 devices in a mesh: row: 16 (over x_hi, y, core), col: 8 (over x_lo, z).
Axes of the slice: x: 4 (x_hi: 2, x_lo: 2; x = x_hi * 2 + x_lo), y: 4, z: 4, core: 2. Of those that a mesh axis runs over, the one named last changes fastest.
Arguments:
- tokens: bfloat16 [512, 512, 384], P('row', 'col'), may hold values from -6 to 6
- w_expand: bfloat16 [384, 1536], replicated, may hold values from -0.3125 to 0.3125
- b_expand: float32 [1536], replicated, may hold values from -3 to 3
- w_depth: float32 [9, 1536], replicated, may hold values from -2 to 2
- b_depth: float32 [1536], replicated, may hold values from -3 to 3
- w_project: bfloat16 [1536, 384], replicated, may hold values from -0.15625 to 0.15625
- w_qkv: bfloat16 [384, 1152], replicated, may hold values from -0.3125 to 0.3125
- w_out: bfloat16 [384, 384], replicated, may hold values from -0.3125 to 0.3125
- pos_table: float32 [12, 225], replicated, may hold values from -3.5 to 320
Outputs:
- mixed: bfloat16 [512, 512, 384], P('row', 'col')
The draws below stay inside these ranges and needn't reach their ends.
All inputs are finite; a program needn't handle non-finite values.
Results may differ from the reference program's by a relative error of at most 0.0065.
Values may be sent and summed in bfloat16 or wider, within the bound.
A program may use at most 128 MiB of HBM per device.

```python
import jax
import jax.numpy as jnp
from jax import lax

HEADS = 12
D = 384
FF = 1536
GRID = 8
H_DEV = 32
NH = 512
NW = 512


def draw_pos_table(key, part):
    key = jax.random.fold_in(key, 7)
    table_span = 2 * GRID - 1
    cell_count = table_span * table_span
    return jnp.clip(jax.random.normal(key, (HEADS, cell_count), jnp.float32), -3.5, 3.5)


def levels(own_key, dims, pieces, low, largest):
    def one(dim, parts):
        steps = jax.random.uniform(jax.random.fold_in(jax.random.fold_in(own_key, 6), dim), (parts,), jnp.float32, low / len(pieces), largest / len(pieces))
        return jnp.repeat(jnp.exp(steps), dims[dim] // parts).reshape((-1,) + (1,) * (len(dims) - dim - 1))

    factor_of = one(*pieces[0])
    for cut in pieces[1:]:
        factor_of = factor_of * one(*cut)
    return factor_of


def gaussian(key, shape, deviation, most, cuts=(), kind=jnp.bfloat16):
    array = jax.random.normal(key, shape, jnp.float32) * deviation
    if len(cuts) > 0:
        array = levels(key, shape, cuts, -0.22, 0.18) * array
    return jnp.clip(array, min=-most, max=most).astype(kind)


def setup_inputs(seed: int = 0) -> dict:
    splits = jax.random.split(jax.random.key(seed), 10)
    return {
        "tokens": gaussian(splits[0], (NH, NW, D), 1.0, 6.0, ((0, 16), (1, 8))),
        "w_expand": gaussian(splits[1], (D, FF), D ** -0.5, 0.3125),
        "b_expand": gaussian(splits[2], (FF,), 0.5, 3.0, (), jnp.float32),
        "w_depth": gaussian(splits[3], (9, FF), 9 ** -0.5, 2.0, (), jnp.float32),
        "b_depth": gaussian(splits[4], (FF,), 0.5, 3.0, (), jnp.float32),
        "w_project": gaussian(splits[5], (FF, D), FF ** -0.5, 0.15625),
        "w_qkv": gaussian(splits[6], (D, 3 * D), D ** -0.5, 0.3125),
        "w_out": gaussian(splits[7], (D, D), D ** -0.5, 0.3125),
        "pos_table": draw_pos_table(jax.random.fold_in(splits[9], 71), 0),
    }


def gelu_tanh(values):
    return jax.nn.gelu(values, approximate=True)

def expand(flat_tokens, w_expand, b_expand):
    preact = jnp.dot(flat_tokens, w_expand, preferred_element_type=jnp.float32) + b_expand
    return gelu_tanh(preact).astype(jnp.bfloat16)

def depth_project(padded_map, centre, w_depth, b_depth, w_project):
    tile_rows, tile_cols, features = centre.shape
    expand_width = padded_map.shape[2]
    conv_sum = jnp.zeros((tile_rows, tile_cols, expand_width), jnp.float32)
    for row_step in range(3):
        for col_step in range(3):
            window = padded_map[row_step:row_step + tile_rows, col_step:col_step + tile_cols].astype(jnp.float32)
            conv_sum = conv_sum + window * w_depth[row_step * 3 + col_step]
    activated = gelu_tanh(conv_sum + b_depth).astype(jnp.bfloat16)
    projected = jnp.dot(activated.reshape(-1, expand_width), w_project, preferred_element_type=jnp.float32)
    merged = centre.reshape(-1, features).astype(jnp.float32) + projected
    return merged.astype(jnp.bfloat16).reshape(tile_rows, tile_cols, features)

def relative_bias(pos_table):
    table_span = 2 * GRID - 1
    places = jnp.arange(GRID * GRID, dtype=jnp.int32)
    row_of = places // GRID
    col_of = places % GRID
    offset = (row_of[:, None] - row_of[None, :] + GRID - 1) * table_span + col_of[:, None] - col_of[None, :] + GRID - 1
    return pos_table[:, offset]

def grid_attention(grouped, w_qkv, w_out, pos_bias):
    group_count, group_size, features = grouped.shape
    head_count = pos_bias.shape[0]
    head_dim = features // head_count
    values = grouped.astype(jnp.float32)
    average = lax.optimization_barrier(jnp.mean(values, axis=-1, keepdims=True))
    centred = values - average
    spread = lax.optimization_barrier(jnp.mean(centred * centred, axis=-1, keepdims=True))
    normed = (centred * lax.rsqrt(spread + 1e-05)).astype(jnp.bfloat16)
    projections = jnp.dot(normed.reshape(-1, features), w_qkv, preferred_element_type=jnp.float32)
    projections = lax.optimization_barrier(projections.astype(jnp.bfloat16)).astype(jnp.float32)
    projections = projections.reshape(group_count, group_size, 3, head_count, head_dim)
    queries = projections[:, :, 0]
    key_rows = projections[:, :, 1]
    value_rows = projections[:, :, 2]
    scores = jnp.einsum('gqhd,gkhd->ghqk', queries, key_rows) * head_dim ** (-0.5) + pos_bias[None]
    peak_score = lax.optimization_barrier(jnp.max(scores, axis=-1, keepdims=True))
    weights = jnp.exp(scores - peak_score)
    soft_weights = weights / lax.optimization_barrier(jnp.sum(weights, axis=-1, keepdims=True))
    soft_weights = lax.optimization_barrier(soft_weights.astype(jnp.bfloat16)).astype(jnp.float32)
    context = jnp.einsum('ghqk,gkhd->gqhd', soft_weights, value_rows).astype(jnp.bfloat16)
    projected = jnp.dot(context.reshape(-1, features), w_out, preferred_element_type=jnp.float32)
    merged = values.reshape(-1, features) + projected
    return merged.astype(jnp.bfloat16).reshape(group_count, group_size, features)

def reference(tokens, w_expand, b_expand, w_depth, b_depth, w_project, w_qkv, w_out, pos_table):
    map_rows, map_cols, features = tokens.shape
    padded_tokens = jnp.pad(tokens, ((1, 1), (0, 0), (0, 0)))

    def one_band(band_index):
        band_start = band_index * H_DEV
        slab = lax.dynamic_slice_in_dim(padded_tokens, band_start, H_DEV + 2, 0)
        grown = expand(slab.reshape(-1, features), w_expand, b_expand).reshape(H_DEV + 2, map_cols, -1)
        row_at = band_start - 1 + jnp.arange(H_DEV + 2, dtype=jnp.int32)
        inside = (row_at >= 0) & (row_at < map_rows)
        grown = jnp.where(inside[:, None, None], grown, jnp.zeros((), jnp.bfloat16))
        padded_map = jnp.pad(grown, ((0, 0), (1, 1), (0, 0)))
        centre = lax.dynamic_slice_in_dim(tokens, band_start, H_DEV, 0)
        return depth_project(padded_map, centre, w_depth, b_depth, w_project)
    bands = lax.map(one_band, jnp.arange(map_rows // H_DEV, dtype=jnp.int32))
    mbconv = bands.reshape(map_rows, map_cols, features)
    row_stride = map_rows // GRID
    col_stride = map_cols // GRID
    by_row = mbconv.reshape(GRID, row_stride, GRID, col_stride, features).transpose(1, 3, 0, 2, 4)
    pos_bias = relative_bias(pos_table)

    def one_line(line_cells):
        grouped = line_cells.reshape(col_stride, GRID * GRID, features)
        result = grid_attention(grouped, w_qkv, w_out, pos_bias)
        return result.reshape(col_stride, GRID, GRID, features)
    finished = lax.map(one_line, by_row)
    return finished.transpose(2, 0, 3, 1, 4).reshape(map_rows, map_cols, features)
```

```python
import functools
import math

import jax
import jax.numpy as jnp
from jax import lax
from jax.experimental import pallas as pl
from jax.experimental.pallas import tpu as pltpu
from jax.sharding import PartitionSpec as P

BF = jnp.bfloat16
F32 = jnp.float32
MESH = pl.DeviceIdType.MESH
D, FF, HEADS, GRID = 384, 1536, 12, 8
C0 = 0.7978845608
C1 = C0 * 0.044715
ALPHA = C1 ** (1.0 / 3.0)
BETA = C0 / ALPHA
LOG2E = 1.4426950408889634
NT = (((1,), (1,)), ((), ()))
TN = (((0,), (0,)), ((), ()))


def dot(a, b):
    return jnp.dot(a, b, preferred_element_type=F32)


def dot_of(a, b, dims):
    return lax.dot_general(a, b, dims, preferred_element_type=F32)


def iota(shape, dim):
    return lax.broadcasted_iota(jnp.int32, shape, dim)


def one_hot(mask):
    return mask.astype(F32).astype(BF)


def swap_8x8():
    p, n = iota((256, 256), 0), iota((256, 256), 1)
    return one_hot(n == (p // 64) * 64 + (p % 8) * 8 + (p // 8) % 8)


def swap_16x16():
    p, n = iota((256, 256), 0), iota((256, 256), 1)
    return one_hot(n == (p % 16) * 16 + p // 16)


def twice_gelu(v):
    t = jnp.tanh(v * (C0 + C1 * (v * v)))
    return v + v * t


def scaled_gelu(z):
    t = jnp.tanh(z * (z * z + BETA))
    return z + z * t


def set_taps(wd, bd, taps):
    for k in range(9):
        taps[k] = jnp.broadcast_to(wd[k : k + 1, :] * (0.5 * ALPHA), (8, FF))
    taps[9] = jnp.broadcast_to(bd[...] * ALPHA, (8, FF))


def permute_rows(tok, swap, perm, first, count):
    def step(c, _):
        x = tok[pl.ds(c * 4, 4)].reshape(256, D)
        perm[pl.ds(c * 4 + 1, 4)] = dot(swap, x).astype(BF).reshape(4, 4, 16, D)
        return 0

    lax.fori_loop(first, first + count, step, 0)


def expand_rows(perm, we, be, grown, r0, n):
    x = perm[pl.ds(r0, n)].reshape(n * 64, D)
    for b in range(6):
        sl = slice(b * 256, b * 256 + 256)
        g = twice_gelu(dot(x, we[:, sl]) + be[:, sl]).reshape(n, 8, 8, 256)
        grown[pl.ds(r0, n), 1:9, :, sl] = g
        for y in range(n):
            grown[r0 + y, 0, :, sl] = pltpu.roll(g[y, 7], 1, 0)
            grown[r0 + y, 9, :, sl] = pltpu.roll(g[y, 0], 7, 0)


def expand_sides(cells, we, be, sides, row, col, rows_last, cols_last):
    ri = iota((80, 1), 0)
    left = (col > 0).astype(F32)
    right = (col < cols_last).astype(F32)
    top = (row > 0).astype(F32)
    bottom = (row < rows_last).astype(F32)
    at = ri % 40
    keep = jnp.where(ri < 40, left, right)
    keep = keep * jnp.where(at == 32, top, 1.0) * jnp.where(at == 33, bottom, 1.0)
    for b in range(6):
        sl = slice(b * 256, b * 256 + 256)
        sides[:, sl] = twice_gelu(dot(cells, we[:, sl]) + be[:, sl]) * keep


def place_sides(sides, grown):
    def step(y, _):
        grown[y + 1, 0, 0:1, :] = sides[pl.ds(y, 1), :]
        grown[y + 1, 9, 7:8, :] = sides[pl.ds(40 + y, 1), :]
        return 0

    lax.fori_loop(0, 32, step, 0)
    for r, at in ((0, 32), (33, 33)):
        grown[r, 0, 0:1, :] = sides[at : at + 1, :]
        grown[r, 9, 7:8, :] = sides[40 + at : 41 + at, :]


def conv_project(perm, grown, taps, wp, out, r0):
    total = None
    for b in range(6):
        parts = []
        for l in range(2):
            sl = slice(b * 256 + l * 128, b * 256 + l * 128 + 128)
            w = [taps[k, :, sl] for k in range(10)]
            done = [[None] * 8 for _ in range(4)]
            for half in range(2):
                sums = [[None] * 4 for _ in range(4)]
                for rr in range(6):
                    e = [grown[r0 + rr, half * 4 + q, :, sl] for q in range(6)]
                    for p in range(3):
                        y = rr - p
                        if not 0 <= y < 4:
                            continue
                        for t in range(4):
                            s = sums[y][t]
                            for q in range(3):
                                m = e[t + q] * w[p * 3 + q]
                                s = w[9] + m if s is None else s + m
                            sums[y][t] = s
                    if rr >= 2:
                        for t in range(4):
                            done[rr - 2][half * 4 + t] = scaled_gelu(sums[rr - 2][t])
            parts.append(jnp.concatenate(sum(done, []), axis=0).astype(BF))
        a = jnp.concatenate(parts, axis=1)
        d = dot(a, wp[b * 256 : b * 256 + 256, :])
        total = d if total is None else total + d
    m = perm[pl.ds(r0 + 1, 4)].reshape(256, D).astype(F32) + total * (0.5 / ALPHA)
    out[pl.ds(r0, 4)] = m.astype(BF).reshape(4, 4, 16, D)


def build_bias(pos, shifts, bias):
    table = jnp.concatenate([pos[...], jnp.zeros((12, 31), F32)], axis=1) * LOG2E
    hi = table.astype(BF)
    rest = table - hi.astype(F32)
    mid = rest.astype(BF)
    low = (rest - mid.astype(F32)).astype(BF)
    c, lane = iota((256, 128), 0), iota((256, 128), 1)
    for js in range(8):
        pick = one_hot(c == (lane // 8) * 15 + lane % 8 - js + 7)
        shifts[:, js, :] = dot(hi, pick) + dot(mid, pick) + dot(low, pick)
    low_half = iota((8, 128), 1) < 64
    for h in range(HEADS):
        x = shifts[h]
        for i in range(8):
            a = pltpu.roll(x, (128 - (7 - i) * 8) % 128, 1)
            b = pltpu.roll(x, (64 + 128 - (7 - i) * 8) % 128, 1)
            bias[h, i * 8 : i * 8 + 8, :] = jnp.where(low_half, a, b)


def group_rows(landed, swap, grouped, normed, sb):
    x = landed[pl.ds(sb * 16, 16)].reshape(256, D)
    v = dot(swap, x)
    grouped[:, pl.ds(sb * 16, 16), :] = v.astype(BF).reshape(16, 16, D)
    centred = v - jnp.mean(v, axis=-1, keepdims=True)
    spread = jnp.mean(centred * centred, axis=-1, keepdims=True)
    y = centred * lax.rsqrt(spread + 1e-05)
    normed[:, pl.ds(sb * 16, 16), :] = y.astype(BF).reshape(16, 16, D)


def project_qkv(normed, wqkv, wvt, qk, vt):
    for c in range(4):
        x = normed[c * 4 : c * 4 + 4].reshape(256, D)
        qk[c * 256 : c * 256 + 256, :] = dot(x, wqkv[:, :768]).astype(BF)
        vt[:, c * 256 : c * 256 + 256] = dot_of(wvt[...], x, NT).astype(BF)


def attend_pair(qk, vt, bias, ctx, at):
    row = iota((256, 128), 0)
    lane = iota((256, 128), 1)
    head_mask = one_hot(row // 64 == lane // 32)
    lo = one_hot(iota((32, 128), 1) < 64)
    hi = one_hot(iota((32, 128), 1) >= 64)
    low_lanes = iota((128, 128), 1) < 64
    none = jnp.zeros((64, 128), BF)
    nothing = jnp.zeros((32, 128), BF)
    scale = LOG2E / math.sqrt(32.0)
    for b in range(3):
        q = qk[pl.ds(at, 128), b * 128 : b * 128 + 128]
        k = qk[pl.ds(at, 128), D + b * 128 : D + b * 128 + 128]
        spread_k = jnp.concatenate(
            [jnp.concatenate([k[g * 64 : g * 64 + 64]] * 4, axis=0) * head_mask for g in range(2)],
            axis=1,
        )
        spread_q = jnp.concatenate(
            [
                jnp.concatenate([q[:64], none], axis=1),
                jnp.concatenate([none, q[64:]], axis=1),
            ],
            axis=0,
        )
        scores = dot_of(spread_k, spread_q, NT)
        weights, inverse = [], []
        for h in range(4):
            s = scores[h * 64 : h * 64 + 64] * scale + bias[b * 4 + h]
            w = jnp.exp2(s - jnp.max(s, axis=0, keepdims=True))
            total = jnp.sum(w, axis=0, keepdims=True)
            inverse.append(jnp.broadcast_to(1.0 / total, (32, 128)))
            weights.append(w.astype(BF))
        weights = jnp.concatenate(weights, axis=0)
        x = vt[b * 128 : b * 128 + 128, pl.ds(at, 128)]
        y = jnp.concatenate([x[:, 64:], x[:, :64]], axis=1)
        rows = []
        for first, second in ((x, y), (y, x)):
            rows.append(jnp.concatenate([first[0:32] * lo, nothing], axis=1))
            rows.append(jnp.concatenate([second[32:64] * hi, nothing], axis=1))
            rows.append(jnp.concatenate([nothing, first[64:96] * lo], axis=1))
            rows.append(jnp.concatenate([nothing, second[96:128] * hi], axis=1))
        both = dot(jnp.concatenate(rows, axis=0), weights)
        mine = jnp.where(low_lanes, both[:128], both[128:])
        mine = mine * jnp.concatenate(inverse, axis=0)
        ctx[b * 128 : b * 128 + 128, pl.ds(at, 128)] = mine.astype(BF)


def project_out(ctx, wout, grouped):
    for c in range(4):
        d = dot_of(ctx[:, c * 256 : c * 256 + 256], wout[...], TN)
        m = grouped[c * 4 : c * 4 + 4].reshape(256, D).astype(F32) + d
        grouped[c * 4 : c * 4 + 4] = m.astype(BF).reshape(4, 64, D)


def ungroup_rows(grouped, swap, out, sb):
    x = grouped[:, pl.ds(sb * 16, 16), :].reshape(256, D)
    out[pl.ds(sb * 16, 16)] = dot(swap, x).astype(BF).reshape(16, 16, D)


def place():
    row, col = lax.axis_index("row"), lax.axis_index("col")
    x = (row // 8) * 2 + col // 4
    return row % 2, x, (row // 2) % 4, col % 4


def device(core, x, y, z):
    return ((x // 2) * 8 + y * 2 + core, (x % 2) * 4 + z)


def slot(x, y, z):
    return ((x // 2) * 4 + y) * 8 + (x % 2) * 4 + z


def mbconv_kernel(tok, rows, cells, we, be, wd, bd, wp, out, perm, grown, sides, taps):
    row, col = lax.axis_index("row"), lax.axis_index("col")
    swap = swap_8x8()
    permute_rows(tok, swap, perm, 0, 8)
    ends = dot(swap[:128, :128], rows[...].reshape(128, D)).astype(BF).reshape(2, 4, 16, D)
    perm[0] = ends[0]
    perm[33] = ends[1]
    set_taps(wd, bd, taps)

    def grow(c, _):
        expand_rows(perm, we, be, grown, c * 4 + 1, 4)
        return 0

    lax.fori_loop(0, 8, grow, 0)
    expand_rows(perm, we, be, grown, 0, 1)
    expand_rows(perm, we, be, grown, 33, 1)

    @pl.when(row == 0)
    def _():
        grown[0] = jnp.zeros(grown.shape[1:], F32)

    @pl.when(row == 15)
    def _():
        grown[33] = jnp.zeros(grown.shape[1:], F32)

    expand_sides(cells[...], we, be, sides, row, col, 15, 7)
    place_sides(sides, grown)

    def mix(c, _):
        conv_project(perm, grown, taps, wp, out, c * 4)
        return 0

    lax.fori_loop(0, 8, mix, 0)


def attention_kernel(landed, wqkv, wout, pos, out, shifts, bias, wvt, grouped, normed, qk, vt, ctx):
    build_bias(pos, shifts, bias)
    eye = one_hot(iota((D, D), 0) == iota((D, D), 1))
    wvt[...] = dot_of(eye, wqkv[:, 768:], NT).astype(BF)
    swap = swap_16x16()
    for h in range(2):
        for sb in range(4):
            group_rows(landed.at[h], swap, grouped, normed, sb)
        project_qkv(normed, wqkv, wvt, qk, vt)

        def pair(n, _):
            attend_pair(qk, vt, bias, ctx, pl.multiple_of(n * 128, 128))
            return 0

        lax.fori_loop(0, 8, pair, 0)
        project_out(ctx, wout, grouped)
        for sb in range(4):
            ungroup_rows(grouped, swap, out.at[h], sb)


OFFSETS = [(a, b, c) for a in (2, 1, 3, 0) for b in (2, 1, 3, 0) for c in (2, 1, 3, 0)][:63]


def exchange_kernel(back, source, out, send_sem, recv_sem, own_sem):
    core, x, y, z = place()
    barrier = pltpu.get_barrier_semaphore()
    for dx, dy, dz in OFFSETS:
        to = device(core, (x + dx) % 4, (y + dy) % 4, (z + dz) % 4)
        pl.semaphore_signal(barrier, inc=1, device_id=to, device_id_type=MESH)
    pl.semaphore_wait(barrier, 63)
    me = slot(x, y, z)

    def ends(h, X, Y, Z):
        if back:
            return source.at[h, slot(X, Y, Z)], out.at[16 * h + 4 * ((x + y + z) % 4) + y, z]
        return source.at[16 * h + 4 * ((X + Y + Z) % 4) + Y, Z], out.at[h, me]

    copies = []
    for h in range(2):
        for n, (dx, dy, dz) in enumerate(OFFSETS):
            X, Y, Z = (x + dx) % 4, (y + dy) % 4, (z + dz) % 4
            src, dst = ends(h, X, Y, Z)
            copy = pltpu.make_async_remote_copy(
                src, dst, send_sem.at[h, n], recv_sem.at[h, n],
                device_id=device(core, X, Y, Z), device_id_type=MESH,
            )
            copy.start()
            copies.append(copy)
        own = pltpu.make_async_copy(*ends(h, x, y, z), own_sem.at[h])
        own.start()
        copies.append(own)
    for copy in copies:
        copy.wait()


def natural_kernel(x, out):
    swap = swap_8x8()

    def step(c, _):
        v = dot(swap, x[pl.ds(c * 4, 4)].reshape(256, D))
        out[pl.ds(c * 4, 4)] = v.astype(BF).reshape(4, 64, D)
        return 0

    lax.fori_loop(0, 8, step, 0)


VM = pl.BlockSpec(memory_space=pltpu.VMEM)
BIG = 58 << 20


def exchange(back, source, shape):
    return pl.pallas_call(
        functools.partial(exchange_kernel, back),
        out_shape=jax.ShapeDtypeStruct(shape, BF),
        in_specs=[VM],
        out_specs=VM,
        scratch_shapes=[
            pltpu.SemaphoreType.DMA((2, 63)),
            pltpu.SemaphoreType.DMA((2, 63)),
            pltpu.SemaphoreType.DMA((2,)),
        ],
        compiler_params=pltpu.CompilerParams(
            collective_id=1 if back else 0, has_side_effects=True, vmem_limit_bytes=BIG
        ),
    )(source)


def shifted(x, axis, step):
    size = lax.axis_size(axis)
    return lax.ppermute(x, axis, [(i, i + step) for i in range(size) if 0 <= i + step < size])


def on_device(tokens, we, be, wd, bd, wp, wqkv, wout, pos):
    top = shifted(tokens[31], "row", 1)
    bottom = shifted(tokens[0], "row", -1)
    rim = lambda c: jnp.concatenate([tokens[:, c], top[c][None], bottom[c][None]], axis=0)
    left = shifted(rim(63), "col", 1)
    right = shifted(rim(0), "col", -1)
    blank = jnp.zeros((6, D), BF)
    cells = jnp.concatenate([left, blank, right, blank], axis=0)
    mb = pl.pallas_call(
        mbconv_kernel,
        out_shape=jax.ShapeDtypeStruct((32, 4, 16, D), BF),
        in_specs=[VM] * 8,
        out_specs=VM,
        scratch_shapes=[
            pltpu.VMEM((34, 4, 16, D), BF),
            pltpu.VMEM((34, 10, 8, FF), F32),
            pltpu.VMEM((80, FF), F32),
            pltpu.VMEM((10, 8, FF), F32),
        ],
        compiler_params=pltpu.CompilerParams(vmem_limit_bytes=BIG),
    )(tokens, jnp.stack([top, bottom]), cells, we, be.reshape(1, FF), wd, bd.reshape(1, FF), wp)
    landed = exchange(False, mb, (2, 64, 16, D))
    result = pl.pallas_call(
        attention_kernel,
        out_shape=jax.ShapeDtypeStruct((2, 64, 16, D), BF),
        in_specs=[VM] * 4,
        out_specs=VM,
        scratch_shapes=[
            pltpu.VMEM((12, 8, 128), F32),
            pltpu.VMEM((12, 64, 128), F32),
            pltpu.VMEM((D, D), BF),
            pltpu.VMEM((16, 64, D), BF),
            pltpu.VMEM((16, 64, D), BF),
            pltpu.VMEM((1024, 768), BF),
            pltpu.VMEM((D, 1024), BF),
            pltpu.VMEM((D, 1024), BF),
        ],
        compiler_params=pltpu.CompilerParams(vmem_limit_bytes=BIG),
    )(landed, wqkv, wout, pos)
    returned = exchange(True, result, (32, 4, 16, D))
    return pl.pallas_call(
        natural_kernel,
        out_shape=jax.ShapeDtypeStruct((32, 64, D), BF),
        in_specs=[VM],
        out_specs=VM,
        compiler_params=pltpu.CompilerParams(vmem_limit_bytes=BIG),
    )(returned)


def solution(mesh):
    placed = (P("row", "col", None), P(), P(), P(), P(), P(), P(), P(), P())
    return jax.shard_map(
        on_device, mesh=mesh, in_specs=placed, out_specs=P("row", "col", None), check_vma=False
    )
```

```python
import functools
import math

import jax
import jax.numpy as jnp
from jax import lax
from jax.experimental import pallas as pl
from jax.experimental.pallas import tpu as pltpu
from jax.sharding import PartitionSpec as P

BF = jnp.bfloat16
F32 = jnp.float32
MESH = pl.DeviceIdType.MESH
D, FF, HEADS, GRID = 384, 1536, 12, 8
C0 = 0.7978845608
C1 = C0 * 0.044715
ALPHA = C1 ** (1.0 / 3.0)
BETA = C0 / ALPHA
LOG2E = 1.4426950408889634
NT = (((1,), (1,)), ((), ()))
TN = (((0,), (0,)), ((), ()))


def dot(a, b):
    return jnp.dot(a, b, preferred_element_type=F32)


def dot_of(a, b, dims):
    return lax.dot_general(a, b, dims, preferred_element_type=F32)


def iota(shape, dim):
    return lax.broadcasted_iota(jnp.int32, shape, dim)


def one_hot(mask):
    return mask.astype(F32).astype(BF)


def swap_8x8():
    p, n = iota((256, 256), 0), iota((256, 256), 1)
    return one_hot(n == (p // 64) * 64 + (p % 8) * 8 + (p // 8) % 8)


def swap_16x16():
    p, n = iota((256, 256), 0), iota((256, 256), 1)
    return one_hot(n == (p % 16) * 16 + p // 16)


def twice_gelu(v):
    t = jnp.tanh(v * (C0 + C1 * (v * v)))
    return v + v * t


def scaled_gelu(z):
    t = jnp.tanh(z * (z * z + BETA))
    return z + z * t


def set_taps(wd, bd, taps):
    for k in range(9):
        taps[k] = jnp.broadcast_to(wd[k : k + 1, :] * (0.5 * ALPHA), (8, FF))
    taps[9] = jnp.broadcast_to(bd[...] * ALPHA, (8, FF))


def permute_rows(tok, swap, perm, edges):
    r, n = iota((64, 256), 0), iota((64, 256), 1)

    def step(c, total):
        x = tok[pl.ds(c * 4, 4)].reshape(256, D)
        perm[pl.ds(c * 4 + 1, 4)] = dot(swap, x).astype(BF).reshape(4, 4, 16, D)
        pick = one_hot(n == (r % 32 - 4 * c) * 64 + (r // 32) * 63)
        return total + dot(pick, x)

    edges[...] = lax.fori_loop(0, 8, step, jnp.zeros((64, D), F32)).astype(BF)


def expand_rows(perm, we, be, grown, r0, n):
    x = perm[pl.ds(r0, n)].reshape(n * 64, D)
    for b in range(6):
        sl = slice(b * 256, b * 256 + 256)
        g = twice_gelu(dot(x, we[:, sl]) + be[:, sl]).reshape(n, 8, 8, 256)
        grown[pl.ds(r0, n), 1:9, :, sl] = g
        for y in range(n):
            grown[r0 + y, 0, :, sl] = pltpu.roll(g[y, 7], 1, 0)
            grown[r0 + y, 9, :, sl] = pltpu.roll(g[y, 0], 7, 0)


def expand_sides(cells, we, be, sides, row, col, rows_last, cols_last):
    ri = iota((128, 1), 0)
    left = (col > 0).astype(F32)
    right = (col < cols_last).astype(F32)
    top = (row > 0).astype(F32)
    bottom = (row < rows_last).astype(F32)
    side = jnp.where(ri < 64, ri // 32, (ri // 16) % 2)
    keep = jnp.where(side == 0, left, right)
    keep = keep * jnp.where(ri < 64, 1.0, jnp.where(ri < 96, top, bottom))
    for b in range(6):
        sl = slice(b * 256, b * 256 + 256)
        sides[:, sl] = twice_gelu(dot(cells, we[:, sl]) + be[:, sl]) * keep


def place_sides(sides, grown):
    def step(y, _):
        grown[y + 1, 0, 0:1, :] = sides[pl.ds(y, 1), :]
        grown[y + 1, 9, 7:8, :] = sides[pl.ds(32 + y, 1), :]
        return 0

    lax.fori_loop(0, 32, step, 0)
    for r, at in ((0, 64), (33, 96)):
        grown[r, 0, 0:1, :] = sides[at + 15 : at + 16, :]
        grown[r, 9, 7:8, :] = sides[at + 16 : at + 17, :]


def conv_project(perm, grown, taps, wp, out, r0):
    total = None
    for b in range(6):
        parts = []
        for l in range(2):
            sl = slice(b * 256 + l * 128, b * 256 + l * 128 + 128)
            w = [taps[k, :, sl] for k in range(10)]
            done = [[None] * 8 for _ in range(4)]
            for half in range(2):
                sums = [[None] * 4 for _ in range(4)]
                for rr in range(6):
                    e = [grown[r0 + rr, half * 4 + q, :, sl] for q in range(6)]
                    for p in range(3):
                        y = rr - p
                        if not 0 <= y < 4:
                            continue
                        for t in range(4):
                            s = sums[y][t]
                            for q in range(3):
                                m = e[t + q] * w[p * 3 + q]
                                s = w[9] + m if s is None else s + m
                            sums[y][t] = s
                    if rr >= 2:
                        for t in range(4):
                            done[rr - 2][half * 4 + t] = scaled_gelu(sums[rr - 2][t])
            parts.append(jnp.concatenate(sum(done, []), axis=0).astype(BF))
        a = jnp.concatenate(parts, axis=1)
        d = dot(a, wp[b * 256 : b * 256 + 256, :])
        total = d if total is None else total + d
    m = perm[pl.ds(r0 + 1, 4)].reshape(256, D).astype(F32) + total * (0.5 / ALPHA)
    out[pl.ds(r0, 4)] = m.astype(BF).reshape(4, 4, 16, D)


def build_bias(pos, shifts, bias):
    table = jnp.concatenate([pos[...], jnp.zeros((12, 31), F32)], axis=1) * LOG2E
    hi = table.astype(BF)
    rest = table - hi.astype(F32)
    mid = rest.astype(BF)
    low = (rest - mid.astype(F32)).astype(BF)
    c, lane = iota((256, 128), 0), iota((256, 128), 1)
    for js in range(8):
        pick = one_hot(c == (lane // 8) * 15 + lane % 8 - js + 7)
        shifts[:, js, :] = dot(hi, pick) + dot(mid, pick) + dot(low, pick)
    low_half = iota((8, 128), 1) < 64
    for h in range(HEADS):
        x = shifts[h]
        for i in range(8):
            a = pltpu.roll(x, (128 - (7 - i) * 8) % 128, 1)
            b = pltpu.roll(x, (64 + 128 - (7 - i) * 8) % 128, 1)
            bias[h, i * 8 : i * 8 + 8, :] = jnp.where(low_half, a, b)


def group_rows(landed, swap, grouped, normed, sb):
    x = landed[pl.ds(sb * 16, 16)].reshape(256, D)
    v = dot(swap, x)
    grouped[:, pl.ds(sb * 16, 16), :] = v.astype(BF).reshape(16, 16, D)
    centred = v - jnp.mean(v, axis=-1, keepdims=True)
    spread = jnp.mean(centred * centred, axis=-1, keepdims=True)
    y = centred * lax.rsqrt(spread + 1e-05)
    normed[:, pl.ds(sb * 16, 16), :] = y.astype(BF).reshape(16, 16, D)


def project_qkv(normed, wqkv, wvt, qk, vt):
    for c in range(4):
        x = normed[c * 4 : c * 4 + 4].reshape(256, D)
        qk[c * 256 : c * 256 + 256, :] = dot(x, wqkv[:, :768]).astype(BF)
        vt[:, c * 256 : c * 256 + 256] = dot_of(wvt[...], x, NT).astype(BF)


def attend_pair(qk, vt, bias, ctx, at):
    row = iota((256, 128), 0)
    lane = iota((256, 128), 1)
    head_mask = one_hot(row // 64 == lane // 32)
    lo = one_hot(iota((32, 128), 1) < 64)
    hi = one_hot(iota((32, 128), 1) >= 64)
    low_lanes = iota((128, 128), 1) < 64
    none = jnp.zeros((64, 128), BF)
    nothing = jnp.zeros((32, 128), BF)
    scale = LOG2E / math.sqrt(32.0)
    for b in range(3):
        q = qk[pl.ds(at, 128), b * 128 : b * 128 + 128]
        k = qk[pl.ds(at, 128), D + b * 128 : D + b * 128 + 128]
        spread_k = jnp.concatenate(
            [jnp.concatenate([k[g * 64 : g * 64 + 64]] * 4, axis=0) * head_mask for g in range(2)],
            axis=1,
        )
        spread_q = jnp.concatenate(
            [
                jnp.concatenate([q[:64], none], axis=1),
                jnp.concatenate([none, q[64:]], axis=1),
            ],
            axis=0,
        )
        scores = dot_of(spread_k, spread_q, NT)
        weights, inverse = [], []
        for h in range(4):
            s = scores[h * 64 : h * 64 + 64] * scale + bias[b * 4 + h]
            w = jnp.exp2(s - jnp.max(s, axis=0, keepdims=True))
            total = jnp.sum(w, axis=0, keepdims=True)
            inverse.append(jnp.broadcast_to(1.0 / total, (32, 128)))
            weights.append(w.astype(BF))
        weights = jnp.concatenate(weights, axis=0)
        x = vt[b * 128 : b * 128 + 128, pl.ds(at, 128)]
        y = jnp.concatenate([x[:, 64:], x[:, :64]], axis=1)
        rows = []
        for first, second in ((x, y), (y, x)):
            rows.append(jnp.concatenate([first[0:32] * lo, nothing], axis=1))
            rows.append(jnp.concatenate([second[32:64] * hi, nothing], axis=1))
            rows.append(jnp.concatenate([nothing, first[64:96] * lo], axis=1))
            rows.append(jnp.concatenate([nothing, second[96:128] * hi], axis=1))
        both = dot(jnp.concatenate(rows, axis=0), weights)
        mine = jnp.where(low_lanes, both[:128], both[128:])
        mine = mine * jnp.concatenate(inverse, axis=0)
        ctx[b * 128 : b * 128 + 128, pl.ds(at, 128)] = mine.astype(BF)


def project_out(ctx, wout, grouped):
    for c in range(4):
        d = dot_of(ctx[:, c * 256 : c * 256 + 256], wout[...], TN)
        m = grouped[c * 4 : c * 4 + 4].reshape(256, D).astype(F32) + d
        grouped[c * 4 : c * 4 + 4] = m.astype(BF).reshape(4, 64, D)


def ungroup_rows(grouped, swap, out, sb):
    x = grouped[:, pl.ds(sb * 16, 16), :].reshape(256, D)
    out[pl.ds(sb * 16, 16)] = dot(swap, x).astype(BF).reshape(16, 16, D)


def place():
    row, col = lax.axis_index("row"), lax.axis_index("col")
    x = (row // 8) * 2 + col // 4
    return row % 2, x, (row // 2) % 4, col % 4


def device(core, x, y, z):
    return ((x // 2) * 8 + y * 2 + core, (x % 2) * 4 + z)


def slot(x, y, z):
    return ((x // 2) * 4 + y) * 8 + (x % 2) * 4 + z


ORDER = [(a, b, c) for a in (2, 1, 3, 0) for b in (2, 1, 3, 0) for c in (2, 1, 3, 0)]
OFFSETS = sorted(ORDER[:63], key=lambda d: -sum(min(k, 4 - k) for k in d))
NEAR = [(1, 0), (-1, 0), (0, 1), (0, -1), (1, 1), (1, -1), (-1, 1), (-1, -1)]


def block_kernel(
    tok, we, be, wd, bd, wp, wqkv, wout, pos, out,
    perm, edges, halo, grown, sides, taps, flat, mb, landed, leaving, back,
    shifts, bias, wvt, grouped, normed, qk, vt, ctx,
    halo_send, halo_recv, go_send, go_recv, back_send, back_recv,
):
    row, col = lax.axis_index("row"), lax.axis_index("col")
    core, x, y, z = place()
    me = slot(x, y, z)

    def beside(dr, dc):
        return (row + dr) % 16, (col + dc) % 8

    barrier = pltpu.get_barrier_semaphore()
    for dr, dc in NEAR:
        if dr != 0:
            pl.semaphore_signal(barrier, inc=1, device_id=beside(dr, dc), device_id_type=MESH)
    for dx, dy, dz in OFFSETS:
        to = device(core, (x + dx) % 4, (y + dy) % 4, (z + dz) % 4)
        pl.semaphore_signal(barrier, inc=1, device_id=to, device_id_type=MESH)

    swap = swap_8x8()
    permute_rows(tok, swap, perm, edges)
    for k in range(12):
        sl = slice(k * 128, k * 128 + 128)
        flat[0:1, sl] = be[sl].reshape(1, 128)
        flat[1:2, sl] = bd[sl].reshape(1, 128)
    pl.semaphore_wait(barrier, 69)

    rims = [
        (tok.at[31], halo.at[0:64], (1, 0)),
        (tok.at[0], halo.at[64:128], (-1, 0)),
        (edges.at[32:64], halo.at[128:160], (0, 1)),
        (edges.at[0:32], halo.at[160:192], (0, -1)),
        (tok.at[31, 48:64], halo.at[192:208], (1, 1)),
        (tok.at[31, 0:16], halo.at[208:224], (1, -1)),
        (tok.at[0, 48:64], halo.at[224:240], (-1, 1)),
        (tok.at[0, 0:16], halo.at[240:256], (-1, -1)),
    ]
    for src, dst, (dr, dc) in rims:
        pltpu.make_async_remote_copy(
            src, dst, halo_send, halo_recv, device_id=beside(dr, dc), device_id_type=MESH
        ).start()

    set_taps(wd, flat.at[1:2], taps)
    bias_row = flat.at[0:1]

    def grow(c, _):
        expand_rows(perm, we, bias_row, grown, c * 4 + 1, 4)
        return 0

    lax.fori_loop(0, 8, grow, 0)
    build_bias(pos, shifts, bias)
    eye = one_hot(iota((D, D), 0) == iota((D, D), 1))
    wvt[...] = dot_of(eye, wqkv[:, 768:], NT).astype(BF)

    pltpu.make_async_copy(halo, halo, halo_recv).wait()
    ends = dot(swap[:128, :128], halo[0:128, :]).astype(BF).reshape(2, 4, 16, D)
    perm[0] = ends[0]
    perm[33] = ends[1]
    expand_rows(perm, we, bias_row, grown, 0, 1)
    expand_rows(perm, we, bias_row, grown, 33, 1)

    @pl.when(row == 0)
    def _():
        grown[0] = jnp.zeros(grown.shape[1:], F32)

    @pl.when(row == 15)
    def _():
        grown[33] = jnp.zeros(grown.shape[1:], F32)

    expand_sides(halo[128:256, :], we, bias_row, sides, row, col, 15, 7)
    place_sides(sides, grown)

    def mix(n, _):
        h, m = n // 4, n % 4
        k = (x + y + z + m) % 4
        conv_project(perm, grown, taps, wp, mb, 16 * h + 4 * k)
        for dy, dz in [(b, c) for b in (2, 1, 3, 0) for c in (2, 1, 3, 0)]:
            Y, Z = (y + dy) % 4, (z + dz) % 4
            X = (k - Y - Z + 8) % 4
            piece = mb.at[16 * h + 4 * k + Y, Z]

            def send():
                pltpu.make_async_remote_copy(
                    piece, landed.at[h, me], go_send.at[h], go_recv.at[h],
                    device_id=device(core, X, Y, Z), device_id_type=MESH,
                ).start()

            if (dy, dz) != (0, 0):
                send()
            else:
                pl.when(m != 0)(send)

                @pl.when(m == 0)
                def _():
                    pltpu.make_async_copy(piece, landed.at[h, me], go_recv.at[h]).start()
        return 0

    lax.fori_loop(0, 8, mix, 0)

    swap16 = swap_16x16()

    def attend(h, _):
        here = landed.at[h]
        pltpu.make_async_copy(here, here, go_recv.at[h]).wait()
        for sb in range(4):
            group_rows(here, swap16, grouped, normed, sb)
        project_qkv(normed, wqkv, wvt, qk, vt)

        def pair(n, _):
            attend_pair(qk, vt, bias, ctx, pl.multiple_of(n * 128, 128))
            return 0

        lax.fori_loop(0, 8, pair, 0)
        project_out(ctx, wout, grouped)
        for sb in range(4):
            ungroup_rows(grouped, swap16, leaving.at[h], sb)
        mine = back.at[16 * h + 4 * ((x + y + z) % 4) + y, z]
        for dx, dy, dz in OFFSETS:
            X, Y, Z = (x + dx) % 4, (y + dy) % 4, (z + dz) % 4
            pltpu.make_async_remote_copy(
                leaving.at[h, slot(X, Y, Z)], mine, back_send.at[h], back_recv.at[h],
                device_id=device(core, X, Y, Z), device_id_type=MESH,
            ).start()
        pltpu.make_async_copy(leaving.at[h, me], mine, back_recv.at[h]).start()
        return 0

    lax.fori_loop(0, 2, attend, 0)

    for h in range(2):
        here = back.at[16 * h : 16 * h + 16]
        pltpu.make_async_copy(here, here, back_recv.at[h]).wait()

        def finish(c, _):
            v = dot(swap, back[pl.ds(c * 4, 4)].reshape(256, D))
            out[pl.ds(c * 4, 4)] = v.astype(BF).reshape(4, 64, D)
            return 0

        lax.fori_loop(4 * h, 4 * h + 4, finish, 0)
    pltpu.make_async_copy(halo, halo, halo_send).wait()
    for h in range(2):
        sent = landed.at[h, 0:63]
        pltpu.make_async_copy(sent, sent, go_send.at[h]).wait()
        pltpu.make_async_copy(sent, sent, back_send.at[h]).wait()


def on_device(tokens, we, be, wd, bd, wp, wqkv, wout, pos):
    vm = pl.BlockSpec(memory_space=pltpu.VMEM)
    shapes = [
        ((34, 4, 16, D), BF), ((64, D), BF), ((256, D), BF), ((34, 10, 8, FF), F32),
        ((128, FF), F32), ((10, 8, FF), F32), ((8, FF), F32), ((32, 4, 16, D), BF),
        ((2, 64, 16, D), BF), ((2, 64, 16, D), BF), ((32, 4, 16, D), BF),
        ((12, 8, 128), F32), ((12, 64, 128), F32), ((D, D), BF), ((16, 64, D), BF),
        ((16, 64, D), BF), ((1024, 768), BF), ((D, 1024), BF), ((D, 1024), BF),
    ]
    dma = pltpu.SemaphoreType.DMA
    return pl.pallas_call(
        block_kernel,
        out_shape=jax.ShapeDtypeStruct((32, 64, D), BF),
        in_specs=[vm] * 9,
        out_specs=vm,
        scratch_shapes=[pltpu.VMEM(*s) for s in shapes]
        + [dma, dma, dma((2,)), dma((2,)), dma((2,)), dma((2,))],
        compiler_params=pltpu.CompilerParams(
            collective_id=0, has_side_effects=True, vmem_limit_bytes=58 << 20
        ),
    )(tokens, we, be, wd, bd, wp, wqkv, wout, pos)


def solution(mesh):
    placed = (P("row", "col", None), P(), P(), P(), P(), P(), P(), P(), P())
    return jax.shard_map(
        on_device, mesh=mesh, in_specs=placed, out_specs=P("row", "col", None), check_vma=False
    )
```

```python
import functools
import math

import jax
import jax.numpy as jnp
from jax import lax
from jax.experimental import pallas as pl
from jax.experimental.pallas import tpu as pltpu
from jax.sharding import PartitionSpec as P

BF = jnp.bfloat16
F32 = jnp.float32
MESH = pl.DeviceIdType.MESH
D, FF, HEADS, GRID = 384, 1536, 12, 8
C0 = 0.7978845608
C1 = C0 * 0.044715
ALPHA = C1 ** (1.0 / 3.0)
BETA = C0 / ALPHA
LOG2E = 1.4426950408889634
NT = (((1,), (1,)), ((), ()))
TN = (((0,), (0,)), ((), ()))


def dot(a, b):
    return jnp.dot(a, b, preferred_element_type=F32)


def dot_of(a, b, dims):
    return lax.dot_general(a, b, dims, preferred_element_type=F32)


def iota(shape, dim):
    return lax.broadcasted_iota(jnp.int32, shape, dim)


def one_hot(mask):
    return mask.astype(F32).astype(BF)


def swap_8x8():
    p, n = iota((256, 256), 0), iota((256, 256), 1)
    return one_hot(n == (p // 64) * 64 + (p % 8) * 8 + (p // 8) % 8)


def swap_16x16():
    p, n = iota((256, 256), 0), iota((256, 256), 1)
    return one_hot(n == (p % 16) * 16 + p // 16)


def twice_gelu(v):
    t = jnp.tanh(v * (C0 + C1 * (v * v)))
    return v + v * t


def scaled_gelu(z):
    t = jnp.tanh(z * (z * z + BETA))
    return z + z * t


def set_taps(wd, bd, taps):
    for k in range(9):
        taps[k] = jnp.broadcast_to(wd[k : k + 1, :] * (0.5 * ALPHA), (8, FF))
    taps[9] = jnp.broadcast_to(bd[...] * ALPHA, (8, FF))


def permute_rows(tok, swap, perm, edges):
    r, n = iota((64, 256), 0), iota((64, 256), 1)

    def step(c, total):
        x = tok[pl.ds(c * 4, 4)].reshape(256, D)
        perm[pl.ds(c * 4 + 1, 4)] = dot(swap, x).astype(BF).reshape(4, 4, 16, D)
        pick = one_hot(n == (r % 32 - 4 * c) * 64 + (r // 32) * 63)
        return total + dot(pick, x)

    edges[...] = lax.fori_loop(0, 8, step, jnp.zeros((64, D), F32)).astype(BF)


def expand_rows(perm, we, be, grown, r0, n):
    x = perm[pl.ds(r0, n)].reshape(n * 64, D)
    for b in range(6):
        sl = slice(b * 256, b * 256 + 256)
        g = twice_gelu(dot(x, we[:, sl]) + be[:, sl]).reshape(n, 8, 8, 256)
        grown[pl.ds(r0, n), 1:9, :, sl] = g
        for y in range(n):
            grown[r0 + y, 0, :, sl] = pltpu.roll(g[y, 7], 1, 0)
            grown[r0 + y, 9, :, sl] = pltpu.roll(g[y, 0], 7, 0)


def expand_sides(cells, we, be, sides, row, col, rows_last, cols_last):
    ri = iota((128, 1), 0)
    left = (col > 0).astype(F32)
    right = (col < cols_last).astype(F32)
    top = (row > 0).astype(F32)
    bottom = (row < rows_last).astype(F32)
    side = jnp.where(ri < 64, ri // 32, (ri // 16) % 2)
    keep = jnp.where(side == 0, left, right)
    keep = keep * jnp.where(ri < 64, 1.0, jnp.where(ri < 96, top, bottom))
    for b in range(6):
        sl = slice(b * 256, b * 256 + 256)
        sides[:, sl] = twice_gelu(dot(cells, we[:, sl]) + be[:, sl]) * keep


def place_sides(sides, grown, first, last):
    def step(y, _):
        grown[y + 1, 0, 0:1, :] = sides[pl.ds(y, 1), :]
        grown[y + 1, 9, 7:8, :] = sides[pl.ds(32 + y, 1), :]
        return 0

    lax.fori_loop(first, last, step, 0)


def place_corners(sides, grown):
    for r, at in ((0, 64), (33, 96)):
        grown[r, 0, 0:1, :] = sides[at + 15 : at + 16, :]
        grown[r, 9, 7:8, :] = sides[at + 16 : at + 17, :]


def conv_project(perm, grown, taps, wp, out, r0):
    total = None
    for b in range(6):
        parts = []
        for l in range(2):
            sl = slice(b * 256 + l * 128, b * 256 + l * 128 + 128)
            w = [taps[k, :, sl] for k in range(10)]
            done = [[None] * 8 for _ in range(4)]
            for half in range(2):
                sums = [[None] * 4 for _ in range(4)]
                for rr in range(6):
                    e = [grown[r0 + rr, half * 4 + q, :, sl] for q in range(6)]
                    for p in range(3):
                        y = rr - p
                        if not 0 <= y < 4:
                            continue
                        for t in range(4):
                            s = sums[y][t]
                            for q in range(3):
                                m = e[t + q] * w[p * 3 + q]
                                s = w[9] + m if s is None else s + m
                            sums[y][t] = s
                    if rr >= 2:
                        for t in range(4):
                            done[rr - 2][half * 4 + t] = scaled_gelu(sums[rr - 2][t])
            parts.append(jnp.concatenate(sum(done, []), axis=0).astype(BF))
        a = jnp.concatenate(parts, axis=1)
        d = dot(a, wp[b * 256 : b * 256 + 256, :])
        total = d if total is None else total + d
    m = perm[pl.ds(r0 + 1, 4)].reshape(256, D).astype(F32) + total * (0.5 / ALPHA)
    out[pl.ds(r0, 4)] = m.astype(BF).reshape(4, 4, 16, D)


def build_bias(pos, shifts, bias):
    table = jnp.concatenate([pos[...], jnp.zeros((12, 31), F32)], axis=1) * LOG2E
    hi = table.astype(BF)
    rest = table - hi.astype(F32)
    mid = rest.astype(BF)
    low = (rest - mid.astype(F32)).astype(BF)
    c, lane = iota((256, 128), 0), iota((256, 128), 1)
    for js in range(8):
        pick = one_hot(c == (lane // 8) * 15 + lane % 8 - js + 7)
        shifts[:, js, :] = dot(hi, pick) + dot(mid, pick) + dot(low, pick)
    low_half = iota((8, 128), 1) < 64
    for h in range(HEADS):
        x = shifts[h]
        for i in range(8):
            a = pltpu.roll(x, (128 - (7 - i) * 8) % 128, 1)
            b = pltpu.roll(x, (64 + 128 - (7 - i) * 8) % 128, 1)
            bias[h, i * 8 : i * 8 + 8, :] = jnp.where(low_half, a, b)


def group_rows(landed, swap, grouped, normed, sb):
    x = landed[pl.ds(sb * 16, 16)].reshape(256, D)
    v = dot(swap, x)
    grouped[:, pl.ds(sb * 16, 16), :] = v.astype(BF).reshape(16, 16, D)
    centred = v - jnp.mean(v, axis=-1, keepdims=True)
    spread = jnp.mean(centred * centred, axis=-1, keepdims=True)
    y = centred * lax.rsqrt(spread + 1e-05)
    normed[:, pl.ds(sb * 16, 16), :] = y.astype(BF).reshape(16, 16, D)


def project_qkv(normed, wqkv, wvt, qk, vt):
    for c in range(4):
        x = normed[c * 4 : c * 4 + 4].reshape(256, D)
        qk[c * 256 : c * 256 + 256, :] = dot(x, wqkv[:, :768]).astype(BF)
        vt[:, c * 256 : c * 256 + 256] = dot_of(wvt[...], x, NT).astype(BF)


def attend_pairs(qk, vt, bias, ctx, places):
    row = iota((256, 128), 0)
    lane = iota((256, 128), 1)
    head_mask = one_hot(row // 64 == lane // 32)
    lo = one_hot(iota((32, 128), 1) < 64)
    hi = one_hot(iota((32, 128), 1) >= 64)
    low_lanes = iota((128, 128), 1) < 64
    none = jnp.zeros((64, 128), BF)
    nothing = jnp.zeros((32, 128), BF)
    scale = LOG2E / math.sqrt(32.0)
    units = [(at, b) for at in places for b in range(3)]
    all_scores = []
    for at, b in units:
        q = qk[pl.ds(at, 128), b * 128 : b * 128 + 128]
        k = qk[pl.ds(at, 128), D + b * 128 : D + b * 128 + 128]
        spread_k = jnp.concatenate(
            [jnp.concatenate([k[g * 64 : g * 64 + 64]] * 4, axis=0) * head_mask for g in range(2)],
            axis=1,
        )
        spread_q = jnp.concatenate(
            [
                jnp.concatenate([q[:64], none], axis=1),
                jnp.concatenate([none, q[64:]], axis=1),
            ],
            axis=0,
        )
        all_scores.append(dot_of(spread_k, spread_q, NT))
    softmaxes = []
    for (at, b), scores in zip(units, all_scores):
        weights, inverse = [], []
        for h in range(4):
            s = scores[h * 64 : h * 64 + 64] * scale + bias[b * 4 + h]
            w = jnp.exp2(s - jnp.max(s, axis=0, keepdims=True))
            total = jnp.sum(w, axis=0, keepdims=True)
            inverse.append(jnp.broadcast_to(1.0 / total, (32, 128)))
            weights.append(w.astype(BF))
        softmaxes.append((jnp.concatenate(weights, axis=0), jnp.concatenate(inverse, axis=0)))
    for (at, b), (weights, inverse) in zip(units, softmaxes):
        x = vt[b * 128 : b * 128 + 128, pl.ds(at, 128)]
        y = jnp.concatenate([x[:, 64:], x[:, :64]], axis=1)
        rows = []
        for first, second in ((x, y), (y, x)):
            rows.append(jnp.concatenate([first[0:32] * lo, nothing], axis=1))
            rows.append(jnp.concatenate([second[32:64] * hi, nothing], axis=1))
            rows.append(jnp.concatenate([nothing, first[64:96] * lo], axis=1))
            rows.append(jnp.concatenate([nothing, second[96:128] * hi], axis=1))
        both = dot(jnp.concatenate(rows, axis=0), weights)
        mine = jnp.where(low_lanes, both[:128], both[128:]) * inverse
        ctx[b * 128 : b * 128 + 128, pl.ds(at, 128)] = mine.astype(BF)


def project_out(ctx, wout, grouped):
    for c in range(4):
        d = dot_of(ctx[:, c * 256 : c * 256 + 256], wout[...], TN)
        m = grouped[c * 4 : c * 4 + 4].reshape(256, D).astype(F32) + d
        grouped[c * 4 : c * 4 + 4] = m.astype(BF).reshape(4, 64, D)


def ungroup_rows(grouped, swap, out, sb):
    x = grouped[:, pl.ds(sb * 16, 16), :].reshape(256, D)
    out[pl.ds(sb * 16, 16)] = dot(swap, x).astype(BF).reshape(16, 16, D)


def place():
    row, col = lax.axis_index("row"), lax.axis_index("col")
    x = (row // 8) * 2 + col // 4
    return row % 2, x, (row // 2) % 4, col % 4


def device(core, x, y, z):
    return ((x // 2) * 8 + y * 2 + core, (x % 2) * 4 + z)


def slot(x, y, z):
    return ((x // 2) * 4 + y) * 8 + (x % 2) * 4 + z


ORDER = [(a, b, c) for a in (2, 1, 3, 0) for b in (2, 1, 3, 0) for c in (2, 1, 3, 0)]
OFFSETS = sorted(ORDER[:63], key=lambda d: -sum(min(k, 4 - k) for k in d))
NEAR = [(1, 0), (-1, 0), (0, 1), (0, -1), (1, 1), (1, -1), (-1, 1), (-1, -1)]


def block_kernel(
    tok_at, we_at, be_at, wd_at, bd_at, wp_at, wqkv_at, wout_at, pos_at, out,
    tok, we, be, wd, bd, wp, wqkv, wout, pos,
    perm, edges, halo, grown, sides, taps, flat, mb, landed, leaving, back,
    shifts, bias, wvt, grouped, normed, qk, vt, ctx,
    load_sem, halo_send, halo_recv, go_send, go_recv, back_send, back_recv, out_sem,
):
    row, col = lax.axis_index("row"), lax.axis_index("col")
    core, x, y, z = place()
    me = slot(x, y, z)
    pairs = [
        (tok_at, tok), (we_at, we), (be_at, be), (pos_at, pos), (wqkv_at, wqkv),
        (wd_at, wd), (bd_at, bd), (wp_at, wp), (wout_at, wout),
    ]
    loads = [pltpu.make_async_copy(a, b, load_sem.at[n]) for n, (a, b) in enumerate(pairs)]
    for load in loads:
        load.start()

    def beside(dr, dc):
        return (row + dr) % 16, (col + dc) % 8

    barrier = pltpu.get_barrier_semaphore()
    for dr, dc in NEAR:
        if dr != 0:
            pl.semaphore_signal(barrier, inc=1, device_id=beside(dr, dc), device_id_type=MESH)
    for dx, dy, dz in OFFSETS:
        to = device(core, (x + dx) % 4, (y + dy) % 4, (z + dz) % 4)
        pl.semaphore_signal(barrier, inc=1, device_id=to, device_id_type=MESH)

    swap = swap_8x8()
    loads[0].wait()
    permute_rows(tok, swap, perm, edges)
    pl.semaphore_wait(barrier, 69)

    rims = [
        (tok.at[31], halo.at[0:64], (1, 0)),
        (tok.at[0], halo.at[64:128], (-1, 0)),
        (edges.at[32:64], halo.at[128:160], (0, 1)),
        (edges.at[0:32], halo.at[160:192], (0, -1)),
        (tok.at[31, 48:64], halo.at[192:208], (1, 1)),
        (tok.at[31, 0:16], halo.at[208:224], (1, -1)),
        (tok.at[0, 48:64], halo.at[224:240], (-1, 1)),
        (tok.at[0, 0:16], halo.at[240:256], (-1, -1)),
    ]
    for src, dst, (dr, dc) in rims:
        pltpu.make_async_remote_copy(
            src, dst, halo_send, halo_recv, device_id=beside(dr, dc), device_id_type=MESH
        ).start()

    for n in range(1, 9):
        loads[n].wait()
    for k in range(12):
        sl = slice(k * 128, k * 128 + 128)
        flat[0:1, sl] = be[sl].reshape(1, 128)
        flat[1:2, sl] = bd[sl].reshape(1, 128)
    set_taps(wd, flat.at[1:2], taps)
    build_bias(pos, shifts, bias)
    eye = one_hot(iota((D, D), 0) == iota((D, D), 1))
    wvt[...] = dot_of(eye, wqkv[:, 768:], NT).astype(BF)
    bias_row = flat.at[0:1]

    def grow(c, _):
        expand_rows(perm, we, bias_row, grown, c * 4 + 1, 4)
        return 0

    lax.fori_loop(0, 5, grow, 0)
    pltpu.make_async_copy(halo, halo, halo_recv).wait()
    ends = dot(swap[:128, :128], halo[0:128, :]).astype(BF).reshape(2, 4, 16, D)
    perm[0] = ends[0]
    perm[33] = ends[1]
    expand_rows(perm, we, bias_row, grown, 0, 1)
    expand_rows(perm, we, bias_row, grown, 33, 1)

    @pl.when(row == 0)
    def _():
        grown[0] = jnp.zeros(grown.shape[1:], F32)

    @pl.when(row == 15)
    def _():
        grown[33] = jnp.zeros(grown.shape[1:], F32)

    expand_sides(halo[128:256, :], we, bias_row, sides, row, col, 15, 7)
    place_sides(sides, grown, 0, 20)
    place_corners(sides, grown)

    def mix(n, _):
        h, m = n // 4, n % 4

        @pl.when(n == 4)
        def _():
            lax.fori_loop(5, 8, grow, 0)
            place_sides(sides, grown, 20, 32)

        k = (x + y + z + m + 1) % 4
        conv_project(perm, grown, taps, wp, mb, 16 * h + 4 * k)
        for dy, dz in [(b, c) for b in (2, 1, 3, 0) for c in (2, 1, 3, 0)]:
            Y, Z = (y + dy) % 4, (z + dz) % 4
            X = (k - Y - Z + 8) % 4
            piece = mb.at[16 * h + 4 * k + Y, Z]

            def send():
                pltpu.make_async_remote_copy(
                    piece, landed.at[h, me], go_send.at[h], go_recv.at[h],
                    device_id=device(core, X, Y, Z), device_id_type=MESH,
                ).start()

            if (dy, dz) != (0, 0):
                send()
            else:
                pl.when(m != 3)(send)

                @pl.when(m == 3)
                def _():
                    pltpu.make_async_copy(piece, landed.at[h, me], go_recv.at[h]).start()
        return 0

    lax.fori_loop(0, 8, mix, 0)

    swap16 = swap_16x16()

    def attend(h, _):
        here = landed.at[h]
        pltpu.make_async_copy(here, here, go_recv.at[h]).wait()
        for sb in range(4):
            group_rows(here, swap16, grouped, normed, sb)
        project_qkv(normed, wqkv, wvt, qk, vt)

        def four(n, _):
            places = [pl.multiple_of(n * 512 + j * 128, 128) for j in range(4)]
            attend_pairs(qk, vt, bias, ctx, places)
            return 0

        lax.fori_loop(0, 2, four, 0)
        project_out(ctx, wout, grouped)
        for sb in range(4):
            ungroup_rows(grouped, swap16, leaving.at[h], sb)
        mine = back.at[16 * h + 4 * ((x + y + z) % 4) + y, z]
        for dx, dy, dz in OFFSETS:
            X, Y, Z = (x + dx) % 4, (y + dy) % 4, (z + dz) % 4
            pltpu.make_async_remote_copy(
                leaving.at[h, slot(X, Y, Z)], mine, back_send.at[h], back_recv.at[h],
                device_id=device(core, X, Y, Z), device_id_type=MESH,
            ).start()
        pltpu.make_async_copy(leaving.at[h, me], mine, back_recv.at[h]).start()
        return 0

    lax.fori_loop(0, 2, attend, 0)
    pltpu.make_async_copy(halo, halo, halo_send).wait()

    outs = []
    for h in range(2):
        here = back.at[16 * h : 16 * h + 16]
        pltpu.make_async_copy(here, here, back_recv.at[h]).wait()
        for c in range(4 * h, 4 * h + 4):
            v = dot(swap, back[c * 4 : c * 4 + 4].reshape(256, D))
            tok[c * 4 : c * 4 + 4] = v.astype(BF).reshape(4, 64, D)
            copy = pltpu.make_async_copy(
                tok.at[c * 4 : c * 4 + 4], out.at[c * 4 : c * 4 + 4], out_sem.at[c]
            )
            copy.start()
            outs.append(copy)
    for h in range(2):
        sent = landed.at[h, 0:63]
        pltpu.make_async_copy(sent, sent, go_send.at[h]).wait()
        pltpu.make_async_copy(sent, sent, back_send.at[h]).wait()
    for copy in outs:
        copy.wait()


def on_device(*args):
    anywhere = pl.BlockSpec(memory_space=pl.ANY)
    shapes = [(a.shape, a.dtype) for a in args]
    shapes += [
        ((34, 4, 16, D), BF), ((64, D), BF), ((256, D), BF), ((34, 10, 8, FF), F32),
        ((128, FF), F32), ((10, 8, FF), F32), ((8, FF), F32), ((32, 4, 16, D), BF),
        ((2, 64, 16, D), BF), ((2, 64, 16, D), BF), ((32, 4, 16, D), BF),
        ((12, 8, 128), F32), ((12, 64, 128), F32), ((D, D), BF), ((16, 64, D), BF),
        ((16, 64, D), BF), ((1024, 768), BF), ((D, 1024), BF), ((D, 1024), BF),
    ]
    dma = pltpu.SemaphoreType.DMA
    return pl.pallas_call(
        block_kernel,
        out_shape=jax.ShapeDtypeStruct((32, 64, D), BF),
        in_specs=[anywhere] * 9,
        out_specs=anywhere,
        scratch_shapes=[pltpu.VMEM(*s) for s in shapes]
        + [dma((9,)), dma, dma, dma((2,)), dma((2,)), dma((2,)), dma((2,)), dma((8,))],
        compiler_params=pltpu.CompilerParams(
            collective_id=0, has_side_effects=True, vmem_limit_bytes=58 << 20
        ),
    )(*args)


def solution(mesh):
    placed = (P("row", "col", None), P(), P(), P(), P(), P(), P(), P(), P())
    return jax.shard_map(
        on_device, mesh=mesh, in_specs=placed, out_specs=P("row", "col", None), check_vma=False
    )
```

```python
import functools
import math

import jax
import jax.numpy as jnp
from jax import lax
from jax.experimental import pallas as pl
from jax.experimental.pallas import tpu as pltpu
from jax.sharding import PartitionSpec as P

BF = jnp.bfloat16
F32 = jnp.float32
MESH = pl.DeviceIdType.MESH
D, FF, HEADS, GRID = 384, 1536, 12, 8
C0 = 0.7978845608
C1 = C0 * 0.044715
ALPHA = C1 ** (1.0 / 3.0)
BETA = C0 / ALPHA
LOG2E = 1.4426950408889634
NT = (((1,), (1,)), ((), ()))
TN = (((0,), (0,)), ((), ()))


def dot(a, b):
    return jnp.dot(a, b, preferred_element_type=F32)


def dot_of(a, b, dims):
    return lax.dot_general(a, b, dims, preferred_element_type=F32)


def iota(shape, dim):
    return lax.broadcasted_iota(jnp.int32, shape, dim)


def one_hot(mask):
    return mask.astype(F32).astype(BF)


def swap_8x8():
    p, n = iota((256, 256), 0), iota((256, 256), 1)
    return one_hot(n == (p // 64) * 64 + (p % 8) * 8 + (p // 8) % 8)


def swap_16x16():
    p, n = iota((256, 256), 0), iota((256, 256), 1)
    return one_hot(n == (p % 16) * 16 + p // 16)


def twice_gelu(v):
    t = jnp.tanh(v * (C0 + C1 * (v * v)))
    return v + v * t


def scaled_gelu(z):
    t = jnp.tanh(z * (z * z + BETA))
    return z + z * t


def set_taps(wd, bd, taps):
    for k in range(9):
        taps[k] = jnp.broadcast_to(wd[k : k + 1, :] * (0.5 * ALPHA), (8, FF))
    taps[9] = jnp.broadcast_to(bd[...] * ALPHA, (8, FF))


def permute_rows(tok, swap, perm, edges):
    r, n = iota((64, 256), 0), iota((64, 256), 1)

    total = jnp.zeros((64, D), F32)
    for c in range(8):
        x = tok[c * 4 : c * 4 + 4].reshape(256, D)
        perm[c * 4 + 1 : c * 4 + 5] = dot(swap, x).astype(BF).reshape(4, 4, 16, D)
        total = total + dot(one_hot(n == (r % 32 - 4 * c) * 64 + (r // 32) * 63), x)
    edges[...] = total.astype(BF)


def expand_rows(perm, we, be, grown, r0, n):
    x = perm[pl.ds(r0, n)].reshape(n * 64, D)
    for b in range(6):
        sl = slice(b * 256, b * 256 + 256)
        g = twice_gelu(dot(x, we[:, sl]) + be[:, sl]).reshape(n, 8, 8, 256)
        for y in range(n):
            for t in range(8):
                grown[r0 + y, 1 + t, :, sl] = g[y, t]
            grown[r0 + y, 0, :, sl] = pltpu.roll(g[y, 7], 1, 0)
            grown[r0 + y, 9, :, sl] = pltpu.roll(g[y, 0], 7, 0)


def expand_sides(cells, we, be, sides, row, col, rows_last, cols_last):
    ri = iota((128, 1), 0)
    left = (col > 0).astype(F32)
    right = (col < cols_last).astype(F32)
    top = (row > 0).astype(F32)
    bottom = (row < rows_last).astype(F32)
    side = jnp.where(ri < 64, ri // 32, (ri // 16) % 2)
    keep = jnp.where(side == 0, left, right)
    keep = keep * jnp.where(ri < 64, 1.0, jnp.where(ri < 96, top, bottom))
    for b in range(6):
        sl = slice(b * 256, b * 256 + 256)
        sides[:, sl] = twice_gelu(dot(cells, we[:, sl]) + be[:, sl]) * keep


def place_sides(sides, grown, first, last):
    def step(y, _):
        grown[y + 1, 0, 0:1, :] = sides[pl.ds(y, 1), :]
        grown[y + 1, 9, 7:8, :] = sides[pl.ds(32 + y, 1), :]
        return 0

    lax.fori_loop(first, last, step, 0)


def place_corners(sides, grown):
    for r, at in ((0, 64), (33, 96)):
        grown[r, 0, 0:1, :] = sides[at + 15 : at + 16, :]
        grown[r, 9, 7:8, :] = sides[at + 16 : at + 17, :]


def conv_project(perm, grown, taps, wp, out, r0):
    total = None
    for b in range(6):
        parts = []
        for l in range(2):
            sl = slice(b * 256 + l * 128, b * 256 + l * 128 + 128)
            w = [taps[k, :, sl] for k in range(10)]
            done = [[None] * 8 for _ in range(4)]
            for half in range(2):
                sums = [[None] * 4 for _ in range(4)]
                for rr in range(6):
                    e = [grown[r0 + rr, half * 4 + q, :, sl] for q in range(6)]
                    for p in range(3):
                        y = rr - p
                        if not 0 <= y < 4:
                            continue
                        for t in range(4):
                            s = sums[y][t]
                            for q in range(3):
                                m = e[t + q] * w[p * 3 + q]
                                s = w[9] + m if s is None else s + m
                            sums[y][t] = s
                    if rr >= 2:
                        for t in range(4):
                            done[rr - 2][half * 4 + t] = scaled_gelu(sums[rr - 2][t])
            parts.append(jnp.concatenate(sum(done, []), axis=0).astype(BF))
        a = jnp.concatenate(parts, axis=1)
        d = dot(a, wp[b * 256 : b * 256 + 256, :])
        total = d if total is None else total + d
    m = perm[pl.ds(r0 + 1, 4)].reshape(256, D).astype(F32) + total * (0.5 / ALPHA)
    out[pl.ds(r0, 4)] = m.astype(BF).reshape(4, 4, 16, D)


def build_bias(pos, shifts, bias):
    table = jnp.concatenate([pos[...], jnp.zeros((12, 31), F32)], axis=1) * LOG2E
    hi = table.astype(BF)
    rest = table - hi.astype(F32)
    mid = rest.astype(BF)
    low = (rest - mid.astype(F32)).astype(BF)
    c, lane = iota((256, 128), 0), iota((256, 128), 1)
    for js in range(8):
        pick = one_hot(c == (lane // 8) * 15 + lane % 8 - js + 7)
        shifts[:, js, :] = dot(hi, pick) + dot(mid, pick) + dot(low, pick)
    low_half = iota((8, 128), 1) < 64
    for h in range(HEADS):
        x = shifts[h]
        for i in range(8):
            a = pltpu.roll(x, (128 - (7 - i) * 8) % 128, 1)
            b = pltpu.roll(x, (64 + 128 - (7 - i) * 8) % 128, 1)
            bias[h, i * 8 : i * 8 + 8, :] = jnp.where(low_half, a, b)


def group_rows(landed, swap, grouped, normed, sb):
    x = landed[pl.ds(sb * 16, 16)].reshape(256, D)
    v = dot(swap, x)
    grouped[:, pl.ds(sb * 16, 16), :] = v.astype(BF).reshape(16, 16, D)
    centred = v - jnp.mean(v, axis=-1, keepdims=True)
    spread = jnp.mean(centred * centred, axis=-1, keepdims=True)
    y = centred * lax.rsqrt(spread + 1e-05)
    normed[:, pl.ds(sb * 16, 16), :] = y.astype(BF).reshape(16, 16, D)


def project_qkv(normed, wqkv, wvt, qk, vt):
    for c in range(4):
        x = normed[c * 4 : c * 4 + 4].reshape(256, D)
        qk[c * 256 : c * 256 + 256, :] = dot(x, wqkv[:, :768]).astype(BF)
        vt[:, c * 256 : c * 256 + 256] = dot_of(wvt[...], x, NT).astype(BF)


def attend_pairs(qk, vt, bias, ctx, places):
    row = iota((256, 128), 0)
    lane = iota((256, 128), 1)
    head_mask = one_hot(row // 64 == lane // 32)
    lo = one_hot(iota((32, 128), 1) < 64)
    hi = one_hot(iota((32, 128), 1) >= 64)
    low_lanes = iota((128, 128), 1) < 64
    none = jnp.zeros((64, 128), BF)
    nothing = jnp.zeros((32, 128), BF)
    scale = LOG2E / math.sqrt(32.0)
    units = [(at, b) for at in places for b in range(3)]
    all_scores = []
    for at, b in units:
        q = qk[pl.ds(at, 128), b * 128 : b * 128 + 128]
        k = qk[pl.ds(at, 128), D + b * 128 : D + b * 128 + 128]
        spread_k = jnp.concatenate(
            [jnp.concatenate([k[g * 64 : g * 64 + 64]] * 4, axis=0) * head_mask for g in range(2)],
            axis=1,
        )
        spread_q = jnp.concatenate(
            [
                jnp.concatenate([q[:64], none], axis=1),
                jnp.concatenate([none, q[64:]], axis=1),
            ],
            axis=0,
        )
        all_scores.append(dot_of(spread_k, spread_q, NT))
    softmaxes = []
    for (at, b), scores in zip(units, all_scores):
        weights, inverse = [], []
        for h in range(4):
            s = scores[h * 64 : h * 64 + 64] * scale + bias[b * 4 + h]
            w = jnp.exp2(s - jnp.max(s, axis=0, keepdims=True))
            total = jnp.sum(w, axis=0, keepdims=True)
            inverse.append(jnp.broadcast_to(1.0 / total, (32, 128)))
            weights.append(w.astype(BF))
        softmaxes.append((jnp.concatenate(weights, axis=0), jnp.concatenate(inverse, axis=0)))
    for (at, b), (weights, inverse) in zip(units, softmaxes):
        x = vt[b * 128 : b * 128 + 128, pl.ds(at, 128)]
        y = jnp.concatenate([x[:, 64:], x[:, :64]], axis=1)
        rows = []
        for first, second in ((x, y), (y, x)):
            rows.append(jnp.concatenate([first[0:32] * lo, nothing], axis=1))
            rows.append(jnp.concatenate([second[32:64] * hi, nothing], axis=1))
            rows.append(jnp.concatenate([nothing, first[64:96] * lo], axis=1))
            rows.append(jnp.concatenate([nothing, second[96:128] * hi], axis=1))
        both = dot(jnp.concatenate(rows, axis=0), weights)
        mine = jnp.where(low_lanes, both[:128], both[128:]) * inverse
        ctx[b * 128 : b * 128 + 128, pl.ds(at, 128)] = mine.astype(BF)


def project_out(ctx, wout, grouped):
    for c in range(4):
        d = dot_of(ctx[:, c * 256 : c * 256 + 256], wout[...], TN)
        m = grouped[c * 4 : c * 4 + 4].reshape(256, D).astype(F32) + d
        grouped[c * 4 : c * 4 + 4] = m.astype(BF).reshape(4, 64, D)


def ungroup_rows(grouped, swap, out, sb):
    x = grouped[:, pl.ds(sb * 16, 16), :].reshape(256, D)
    out[pl.ds(sb * 16, 16)] = dot(swap, x).astype(BF).reshape(16, 16, D)


def place():
    row, col = lax.axis_index("row"), lax.axis_index("col")
    x = lax.div(row, 8) * 2 + lax.div(col, 4)
    return lax.rem(row, 2), x, lax.rem(lax.div(row, 2), 4), lax.rem(col, 4)


def along_x(x):
    high, low = lax.div(x, 2), lax.rem(x, 2)
    return high * 8, low * 4, high * 32 + low * 4


ORDER = [(a, b, c) for a in (2, 1, 3, 0) for b in (2, 1, 3, 0) for c in (2, 1, 3, 0)]
OFFSETS = sorted(ORDER[:63], key=lambda d: -sum(min(k, 4 - k) for k in d))
NEAR = [(1, 0), (-1, 0), (0, 1), (0, -1), (1, 1), (1, -1), (-1, 1), (-1, -1)]


def block_kernel(
    tok_at, we_at, be_at, wd_at, bd_at, wp_at, wqkv_at, wout_at, pos_at, out,
    tok, we, be, wd, bd, wp, wqkv, wout, pos,
    perm, edges, halo, grown, sides, taps, flat, mb, landed, leaving, back,
    shifts, bias, wvt, grouped, normed, qk, vt, ctx,
    load_sem, halo_send, halo_recv, go_send, go_recv, back_send, back_recv, out_sem,
):
    row, col = lax.axis_index("row"), lax.axis_index("col")
    core, x, y, z = place()
    xs = [along_x(lax.rem(x + d, 4)) for d in range(4)]
    ys = [lax.rem(y + d, 4) for d in range(4)]
    zs = [lax.rem(z + d, 4) for d in range(4)]
    rows_of = [2 * a + core for a in ys]
    slots_of = [8 * a for a in ys]
    me = xs[0][2] + 8 * y + z

    def offset_device(dx, dy, dz):
        return xs[dx][0] + rows_of[dy], xs[dx][1] + zs[dz]

    pairs = [
        (tok_at, tok), (we_at, we), (be_at, be), (pos_at, pos), (wqkv_at, wqkv),
        (wd_at, wd), (bd_at, bd), (wp_at, wp), (wout_at, wout),
    ]
    loads = [pltpu.make_async_copy(a, b, load_sem.at[n]) for n, (a, b) in enumerate(pairs)]
    for load in loads:
        load.start()

    def beside(dr, dc):
        return lax.rem(row + dr + 16, 16), lax.rem(col + dc + 8, 8)

    barrier = pltpu.get_barrier_semaphore()
    for dr, dc in NEAR:
        if dr != 0:
            pl.semaphore_signal(barrier, inc=1, device_id=beside(dr, dc), device_id_type=MESH)
    for dx, dy, dz in OFFSETS:
        to = offset_device(dx, dy, dz)
        pl.semaphore_signal(barrier, inc=1, device_id=to, device_id_type=MESH)

    swap = swap_8x8()
    loads[0].wait()
    permute_rows(tok, swap, perm, edges)
    pl.semaphore_wait(barrier, 69)

    rims = [
        (tok.at[31], halo.at[0:64], (1, 0)),
        (tok.at[0], halo.at[64:128], (-1, 0)),
        (edges.at[32:64], halo.at[128:160], (0, 1)),
        (edges.at[0:32], halo.at[160:192], (0, -1)),
        (tok.at[31, 48:64], halo.at[192:208], (1, 1)),
        (tok.at[31, 0:16], halo.at[208:224], (1, -1)),
        (tok.at[0, 48:64], halo.at[224:240], (-1, 1)),
        (tok.at[0, 0:16], halo.at[240:256], (-1, -1)),
    ]
    for src, dst, (dr, dc) in rims:
        pltpu.make_async_remote_copy(
            src, dst, halo_send, halo_recv, device_id=beside(dr, dc), device_id_type=MESH
        ).start()

    for n in range(1, 9):
        loads[n].wait()
    for k in range(12):
        sl = slice(k * 128, k * 128 + 128)
        flat[0:1, sl] = be[sl].reshape(1, 128)
        flat[1:2, sl] = bd[sl].reshape(1, 128)
    set_taps(wd, flat.at[1:2], taps)
    build_bias(pos, shifts, bias)
    eye = one_hot(iota((D, D), 0) == iota((D, D), 1))
    wvt[...] = dot_of(eye, wqkv[:, 768:], NT).astype(BF)
    bias_row = flat.at[0:1]

    expand_rows(perm, we, bias_row, grown, 1, 16)
    expand_rows(perm, we, bias_row, grown, 17, 4)
    pltpu.make_async_copy(halo, halo, halo_recv).wait()
    ends = dot(swap[:128, :128], halo[0:128, :]).astype(BF).reshape(2, 4, 16, D)
    perm[0] = ends[0]
    perm[33] = ends[1]
    expand_rows(perm, we, bias_row, grown, 0, 1)
    expand_rows(perm, we, bias_row, grown, 33, 1)

    @pl.when(row == 0)
    def _():
        grown[0] = jnp.zeros(grown.shape[1:], F32)

    @pl.when(row == 15)
    def _():
        grown[33] = jnp.zeros(grown.shape[1:], F32)

    expand_sides(halo[128:256, :], we, bias_row, sides, row, col, 15, 7)
    place_sides(sides, grown, 0, 20)
    place_corners(sides, grown)

    def mix(n, _):
        h, m = lax.div(n, 4), lax.rem(n, 4)

        @pl.when(n == 4)
        def _():
            expand_rows(perm, we, bias_row, grown, 21, 12)
            place_sides(sides, grown, 20, 32)

        first = 16 * h + 4 * lax.rem(x + y + z + m + 1, 4)
        conv_project(perm, grown, taps, wp, mb, first)
        targets = [along_x(lax.rem(x + m + 5 - d, 4)) for d in range(4)]
        for dy, dz in [(b, c) for b in (2, 1, 3, 0) for c in (2, 1, 3, 0)]:
            X = targets[(dy + dz) % 4]
            piece = mb.at[first + ys[dy], zs[dz]]
            to = (X[0] + rows_of[dy], X[1] + zs[dz])

            def send():
                pltpu.make_async_remote_copy(
                    piece, landed.at[h, me], go_send.at[h], go_recv.at[h],
                    device_id=to, device_id_type=MESH,
                ).start()

            if (dy, dz) != (0, 0):
                send()
            else:
                pl.when(m != 3)(send)

                @pl.when(m == 3)
                def _():
                    pltpu.make_async_copy(piece, landed.at[h, me], go_recv.at[h]).start()
        return 0

    lax.fori_loop(0, 8, mix, 0)

    swap16 = swap_16x16()

    def attend(h, _):
        here = landed.at[h]
        pltpu.make_async_copy(here, here, go_recv.at[h]).wait()
        for sb in range(4):
            group_rows(here, swap16, grouped, normed, sb)
        project_qkv(normed, wqkv, wvt, qk, vt)

        def four(n, _):
            places = [pl.multiple_of(n * 512 + j * 128, 128) for j in range(4)]
            attend_pairs(qk, vt, bias, ctx, places)
            return 0

        lax.fori_loop(0, 2, four, 0)
        project_out(ctx, wout, grouped)
        for sb in range(4):
            ungroup_rows(grouped, swap16, leaving.at[h], sb)
        mine = back.at[16 * h + 4 * lax.rem(x + y + z, 4) + y, z]
        for dx, dy, dz in OFFSETS:
            theirs = xs[dx][2] + slots_of[dy] + zs[dz]
            pltpu.make_async_remote_copy(
                leaving.at[h, theirs], mine, back_send.at[h], back_recv.at[h],
                device_id=offset_device(dx, dy, dz), device_id_type=MESH,
            ).start()
        pltpu.make_async_copy(leaving.at[h, me], mine, back_recv.at[h]).start()
        return 0

    lax.fori_loop(0, 2, attend, 0)
    pltpu.make_async_copy(halo, halo, halo_send).wait()

    outs = []
    for h in range(2):
        here = back.at[16 * h : 16 * h + 16]
        pltpu.make_async_copy(here, here, back_recv.at[h]).wait()
        for c in range(4 * h, 4 * h + 4):
            v = dot(swap, back[c * 4 : c * 4 + 4].reshape(256, D))
            tok[c * 4 : c * 4 + 4] = v.astype(BF).reshape(4, 64, D)
            copy = pltpu.make_async_copy(
                tok.at[c * 4 : c * 4 + 4], out.at[c * 4 : c * 4 + 4], out_sem.at[c]
            )
            copy.start()
            outs.append(copy)
    for h in range(2):
        sent = landed.at[h, 0:63]
        pltpu.make_async_copy(sent, sent, go_send.at[h]).wait()
        pltpu.make_async_copy(sent, sent, back_send.at[h]).wait()
    for copy in outs:
        copy.wait()


def on_device(*args):
    anywhere = pl.BlockSpec(memory_space=pl.ANY)
    shapes = [(a.shape, a.dtype) for a in args]
    shapes += [
        ((34, 4, 16, D), BF), ((64, D), BF), ((256, D), BF), ((34, 10, 8, FF), F32),
        ((128, FF), F32), ((10, 8, FF), F32), ((8, FF), F32), ((32, 4, 16, D), BF),
        ((2, 64, 16, D), BF), ((2, 64, 16, D), BF), ((32, 4, 16, D), BF),
        ((12, 8, 128), F32), ((12, 64, 128), F32), ((D, D), BF), ((16, 64, D), BF),
        ((16, 64, D), BF), ((1024, 768), BF), ((D, 1024), BF), ((D, 1024), BF),
    ]
    dma = pltpu.SemaphoreType.DMA
    return pl.pallas_call(
        block_kernel,
        out_shape=jax.ShapeDtypeStruct((32, 64, D), BF),
        in_specs=[anywhere] * 9,
        out_specs=anywhere,
        scratch_shapes=[pltpu.VMEM(*s) for s in shapes]
        + [dma((9,)), dma, dma, dma((2,)), dma((2,)), dma((2,)), dma((2,)), dma((8,))],
        compiler_params=pltpu.CompilerParams(
            collective_id=0, has_side_effects=True, vmem_limit_bytes=58 << 20
        ),
    )(*args)


def solution(mesh):
    placed = (P("row", "col", None), P(), P(), P(), P(), P(), P(), P(), P())
    return jax.shard_map(
        on_device, mesh=mesh, in_specs=placed, out_specs=P("row", "col", None), check_vma=False
    )
```
